32 devices in a mesh: dp: 8 (over y, x, core), tensor: 4 (over z).
Axes of the slice: x: 2, y: 2, z: 4, core: 2. Of those that a mesh axis runs over, the one named last changes fastest.
Arguments:
- hidden_in: bfloat16 [8192, 1024], P(('dp', 'tensor')), may hold values from -6 to 6
- out_grad: bfloat16 [8192, 1024], P(('dp', 'tensor')), may hold values from -6 to 6
- seg_ids: int32 [8192], replicated, may hold values from 0 to 8, as said below
- norm_gain: float32 [1024], replicated, may hold values from 0.1 to 1.9
- gate_weight: bfloat16 [1024, 2048], P('dp', 'tensor'), may hold values from -0.1875 to 0.1875
- value_weight: bfloat16 [1024, 2048], P('dp', 'tensor'), may hold values from -0.1875 to 0.1875
- write_weight: bfloat16 [1024, 128], P('dp', 'tensor'), may hold values from -0.1875 to 0.1875
- read_weight: bfloat16 [1024, 128], P('dp', 'tensor'), may hold values from -0.1875 to 0.1875
- step_weight: bfloat16 [1024, 32], P('dp', 'tensor'), may hold values from -0.1875 to 0.1875
- step_bias: float32 [32], P('tensor'), may hold values from -3 to -1
- decay_log: float32 [32], P('tensor')
- skip_gain: float32 [32], P('tensor'), may hold values from 0.5 to 1.5
- conv_value: float32 [4, 2048], P(None, 'tensor'), may hold values from -3 to 3
- conv_write_read: float32 [2, 4, 128], P(None, None, 'tensor'), may hold values from -3 to 3
- conv_value_bias: float32 [2048], P('tensor'), may hold values from -3 to 3
- conv_write_read_bias: float32 [2, 128], P(None, 'tensor'), may hold values from -3 to 3
- gate_gain: float32 [2048], P('tensor'), may hold values from 0.1 to 1.9
- out_weight: bfloat16 [1024, 2048], P('dp', 'tensor'), may hold values from -0.125 to 0.125
Outputs:
- layer_out: float32 [8192, 1024], P(('dp', 'tensor'))
- input_grad: float32 [8192, 1024], P(('dp', 'tensor'))
- grad_norm_gain: float32 [1024], P('tensor')
- grad_gate_weight: float32 [1024, 2048], P('dp', 'tensor')
- grad_value_weight: float32 [1024, 2048], P('dp', 'tensor')
- grad_write_weight: float32 [1024, 128], P('dp', 'tensor')
- grad_read_weight: float32 [1024, 128], P('dp', 'tensor')
- grad_step_weight: float32 [1024, 32], P('dp', 'tensor')
- grad_step_bias: float32 [32], P('tensor')
- grad_decay_log: float32 [32], P('tensor')
- grad_skip_gain: float32 [32], P('tensor')
- grad_conv_value: float32 [4, 2048], P(None, 'tensor')
- grad_conv_write_read: float32 [2, 4, 128], P(None, None, 'tensor')
- grad_conv_value_bias: float32 [2048], P('tensor')
- grad_conv_write_read_bias: float32 [2, 128], P(None, 'tensor')
- grad_gate_gain: float32 [2048], P('tensor')
- grad_out_weight: float32 [1024, 2048], P('dp', 'tensor')
The draws below stay inside these ranges and needn't reach their ends.
Inputs may be any that keep to these rules, and one draw needn't show every extreme that they name: `seg_ids`: never falls along the tokens and rises by one where a sequence starts; each block of 1024 tokens holds exactly one start of a sequence away from its first token, so a sequence continues into every block from the one before.
All inputs are finite; a program needn't handle non-finite values.
Results may differ from the reference program's by a relative error of at most 0.0021.
The reference program's roundings to bfloat16 on the way count: a program that leaves them out, or rounds other values in their place, can miss the bound.
Values may be sent and summed in bfloat16 or wider, within the bound.
A program may use at most 192 MiB of HBM per device.

```python
import math
import jax
import jax.numpy as jnp
from jax import lax

D = 1024
HEADS = 32
HEADDIM = 64
STATE = 128
CONV_W = 4
SPAN = 256
TOK_GROUP = 1024
TOKENS = 8192


def draw_seg_ids(key, part):
    key = jax.random.fold_in(key, 3)
    groups = TOKENS // TOK_GROUP
    inside = jax.random.randint(key, (groups,), TOK_GROUP // 4, 3 * TOK_GROUP // 4 + 1)
    starts = jnp.arange(groups, dtype=jnp.int32) * TOK_GROUP + inside
    position = jnp.arange(TOKENS, dtype=jnp.int32)
    number = jnp.sum((position[None, :] >= starts[:, None]).astype(jnp.int32), axis=0)
    return number.astype(jnp.int32)


def draw_decay_log(key, part):
    key = jax.random.fold_in(key, 7)
    spread = jax.random.uniform(key, (HEADS,), jnp.float32)
    lowest = math.log(0.01 / TOKENS)
    top_rate = math.log(0.2)
    return (lowest + spread * (top_rate - lowest)).astype(jnp.float32)


def level_of(rng, shape, cuts, least, largest):
    gain, own = 1.0, jax.random.fold_in(rng, 6)
    for dim, shards_of in cuts:
        heights = jnp.exp(jax.random.uniform(jax.random.fold_in(own, dim), (shards_of,), jnp.float32, least / len(cuts), largest / len(cuts)))
        gain = gain * jnp.repeat(heights, shape[dim] // shards_of).reshape([-1 if axis == dim else 1 for axis in range(len(shape))])
    return gain


def centred(own_key, extent, scale, reach, cuts=(), kind=jnp.bfloat16):
    values = jax.random.normal(own_key, extent, jnp.float32) * scale
    if len(cuts) > 0:
        values = level_of(own_key, extent, cuts, -0.22, 0.18) * values
    return jnp.clip(values, min=-reach, max=reach).astype(kind)


def setup_inputs(seed: int = 0) -> dict:
    streams_of = jax.random.split(jax.random.key(seed), 19)
    hidden_in = centred(streams_of[0], (TOKENS, D), 1.0, 6.0, ((0, 32),))
    out_grad = centred(streams_of[1], (TOKENS, D), 1.0, 6.0, ((0, 32),))
    seg_ids = draw_seg_ids(jax.random.fold_in(streams_of[18], 71), 0)
    norm_gain = jnp.clip(1.0 + 0.18 * jax.random.normal(streams_of[3], (D,), jnp.float32), 0.1, 1.9)
    gate_weight = centred(streams_of[4], (D, HEADS * HEADDIM), D ** -0.5, 0.1875, ((0, 8), (1, 4)))
    value_weight = centred(streams_of[5], (D, HEADS * HEADDIM), D ** -0.5, 0.1875, ((0, 8), (1, 4)))
    write_weight = centred(streams_of[6], (D, STATE), D ** -0.5, 0.1875, ((0, 8), (1, 4)))
    read_weight = centred(streams_of[7], (D, STATE), D ** -0.5, 0.1875, ((0, 8), (1, 4)))
    step_weight = centred(streams_of[8], (D, HEADS), D ** -0.5, 0.1875, ((0, 8), (1, 4)))
    step_bias = jnp.clip(-3.0 + 2.0 * jax.random.uniform(streams_of[9], (HEADS,), jnp.float32) ** level_of(streams_of[9], (HEADS,), ((0, 4),), -0.2, 0.2), -3.0, -1.0)
    decay_log = draw_decay_log(jax.random.fold_in(streams_of[18], 71), 0)
    skip_gain = jnp.clip(0.5 + 1.0 * jax.random.uniform(streams_of[11], (HEADS,), jnp.float32) ** level_of(streams_of[11], (HEADS,), ((0, 4),), -0.2, 0.2), 0.5, 1.5)
    conv_value = centred(streams_of[12], (CONV_W, HEADS * HEADDIM), CONV_W ** -0.5, 3.0, ((1, 4),), jnp.float32)
    conv_write_read = centred(streams_of[13], (2, CONV_W, STATE), CONV_W ** -0.5, 3.0, ((2, 4),), jnp.float32)
    conv_value_bias = centred(streams_of[14], (HEADS * HEADDIM,), 0.5, 3.0, ((0, 4),), jnp.float32)
    conv_write_read_bias = centred(streams_of[15], (2, STATE), 0.5, 3.0, ((1, 4),), jnp.float32)
    gate_gain = jnp.clip(1.0 + 0.18 * jax.random.normal(streams_of[16], (HEADS * HEADDIM,), jnp.float32), 0.1, 1.9)
    out_weight = centred(streams_of[17], (D, HEADS * HEADDIM), (HEADS * HEADDIM) ** -0.5, 0.125, ((0, 8), (1, 4)))
    return dict(hidden_in=hidden_in, out_grad=out_grad, seg_ids=seg_ids, norm_gain=norm_gain, gate_weight=gate_weight, value_weight=value_weight, write_weight=write_weight, read_weight=read_weight, step_weight=step_weight, step_bias=step_bias, decay_log=decay_log, skip_gain=skip_gain, conv_value=conv_value, conv_write_read=conv_write_read, conv_value_bias=conv_value_bias, conv_write_read_bias=conv_write_read_bias, gate_gain=gate_gain, out_weight=out_weight)


epsilon = 1e-05
highest = lax.Precision.HIGHEST

@jax.custom_vjp
def low(v):
    return lax.optimization_barrier(v.astype(jnp.bfloat16)).astype(jnp.float32)

@jax.custom_vjp
def low_back(v):
    return v

def low_keep(v):
    return (low(v), None)

def low_pass(kept, grad):
    return (grad,)

def back_keep(v):
    return (v, None)

def back_low(kept, grad):
    return (low(grad),)
low.defvjp(low_keep, low_pass)
low_back.defvjp(back_keep, back_low)

def matmul(left, right):
    return jnp.dot(left, right, precision=highest, preferred_element_type=jnp.float32)

def span_terms(state, before, values, writes, reads, steps, logs, segment):
    length = segment.shape[0]
    order = jnp.arange(length)
    running = jnp.cumsum(logs, axis=0)
    same = (segment[:, None] == segment[None, :]) & (order[:, None] >= order[None, :])
    gap = running[:, None, :] - running[None, :, :]
    decay = jnp.exp(jnp.where(same[:, :, None], gap, -1e+30))
    scores = jnp.dot(reads, writes.T, precision=highest)
    mixing = decay * scores[:, :, None] * steps[None, :, :]
    inner_out = jnp.einsum('tsh,shp->thp', mixing, values, precision=highest)
    carried = segment == before
    entry = jnp.where(carried[:, None], jnp.exp(running), 0.0)
    outer_out = entry[:, :, None] * jnp.einsum('tn,hpn->thp', reads, state, precision=highest)
    ending = segment == segment[-1]
    to_end = jnp.where(ending[:, None], jnp.exp(running[-1][None, :] - running), 0.0) * steps
    written = jnp.einsum('sh,shp,sn->hpn', to_end, values, writes, precision=highest)
    return (entry[-1][:, None, None] * state + written, inner_out + outer_out)

def scan_mixer(values, writes, reads, steps, logs, segment):
    total_rows, heads, head_size = values.shape
    state_size = writes.shape[1]
    count = total_rows // SPAN
    checked = jax.checkpoint(span_terms)

    def span_step(carry, block):
        state, before = carry
        state_new, block_out = checked(state, before, *block)
        return ((state_new, block[-1][-1]), block_out)
    blocks = tuple((item.reshape((count, SPAN) + item.shape[1:]) for item in (values, writes, reads, steps, logs, segment)))
    start = (jnp.zeros((heads, head_size, state_size), jnp.float32), jnp.array(-1, jnp.int32))
    _, outputs = lax.scan(span_step, start, blocks)
    return outputs.reshape(values.shape)

def layer(hidden, norm_gain, gate_weight, value_weight, write_weight, read_weight, step_weight, step_bias, decay_log, skip_gain, conv_value, conv_write_read, conv_value_bias, conv_write_read_bias, gate_gain, out_weight, seg_ids):
    total_rows = hidden.shape[0]
    inner = value_weight.shape[1]
    state_size = write_weight.shape[1]
    heads = step_weight.shape[1]
    head_size = inner // heads
    width = conv_value.shape[0]
    scale = lax.rsqrt(lax.optimization_barrier(jnp.mean(hidden * hidden, axis=1, keepdims=True)) + epsilon)
    features = low(hidden * scale * norm_gain[None, :])
    gate_in = low_back(matmul(features, gate_weight))
    conv_in = jnp.concatenate([low_back(matmul(features, value_weight)), low_back(matmul(features, write_weight)), low_back(matmul(features, read_weight))], axis=1)
    step_in = low_back(matmul(features, step_weight))
    kernel = jnp.concatenate([conv_value, conv_write_read[0], conv_write_read[1]], axis=1)
    offset = jnp.concatenate([conv_value_bias, conv_write_read_bias[0], conv_write_read_bias[1]])
    padded_seg = jnp.concatenate([jnp.full((width - 1,), -1, jnp.int32), seg_ids])
    padded_in = jnp.concatenate([jnp.zeros((width - 1, conv_in.shape[1]), jnp.float32), conv_in], axis=0)
    total = offset[None, :]
    for tap_index in range(width):
        begin = width - 1 - tap_index
        valid = padded_seg[begin:begin + total_rows] == seg_ids
        total = total + kernel[tap_index][None, :] * jnp.where(valid[:, None], padded_in[begin:begin + total_rows], 0.0)
    acted = jax.nn.silu(total)
    values = acted[:, :inner].reshape(total_rows, heads, head_size)
    writes = low(acted[:, inner:inner + state_size])
    reads = low(acted[:, inner + state_size:])
    steps = jax.nn.softplus(step_in + step_bias[None, :])
    logs = -jnp.exp(decay_log)[None, :] * steps
    mixed = scan_mixer(values, writes, reads, steps, logs, seg_ids) + skip_gain[None, :, None] * values
    gated = mixed.reshape(total_rows, inner) * jax.nn.silu(gate_in)
    rms = lax.rsqrt(lax.optimization_barrier(jnp.mean(gated * gated, axis=1, keepdims=True)) + epsilon)
    branch = low(gated * rms * gate_gain[None, :])
    return hidden + matmul(branch, out_weight.T)

def reference(hidden_in, out_grad, seg_ids, norm_gain, gate_weight, value_weight, write_weight, read_weight, step_weight, step_bias, decay_log, skip_gain, conv_value, conv_write_read, conv_value_bias, conv_write_read_bias, gate_gain, out_weight):
    params = (hidden_in.astype(jnp.float32), norm_gain, gate_weight.astype(jnp.float32), value_weight.astype(jnp.float32), write_weight.astype(jnp.float32), read_weight.astype(jnp.float32), step_weight.astype(jnp.float32), step_bias, decay_log, skip_gain, conv_value, conv_write_read, conv_value_bias, conv_write_read_bias, gate_gain, out_weight.astype(jnp.float32))

    def wrapped(*inputs):
        return layer(*inputs, seg_ids)
    layer_out, backward = jax.vjp(wrapped, *params)
    grads = backward(out_grad.astype(jnp.float32))
    return (layer_out, grads[0], grads[1], grads[2], grads[3], grads[4], grads[5], grads[6], grads[7], grads[8], grads[9], grads[10], grads[11], grads[12], grads[13], grads[14], grads[15])
```

```python
from functools import partial

import jax
import jax.numpy as jnp
from jax import lax
from jax.experimental import pallas as pl
from jax.experimental.pallas import tpu as pltpu
from jax.sharding import PartitionSpec as P

SPAN = 128


epsilon = 1e-05
highest = lax.Precision.HIGHEST


def from_behind(value, axis, steps):
    count = lax.axis_size(axis)
    leading, last = (max(0, -steps), min(count, count - steps))
    return lax.ppermute(value, axis, [(source, source + steps) for source in range(leading, last)])


def product(left, right, left_dim=1, right_dim=0):
    return lax.dot_general(
        left, right, (((left_dim,), (right_dim,)), ((), ())), preferred_element_type=jnp.float32
    )


def pieces_of(value, count):
    pieces = []
    for _ in range(count - 1):
        piece = value.astype(jnp.bfloat16)
        pieces.append(piece)
        value = value - piece.astype(jnp.float32)
    return pieces + [value.astype(jnp.bfloat16)]


def exact_left(left, right, count, left_dim=1, right_dim=0):
    return sum(product(left, piece, left_dim, right_dim) for piece in pieces_of(right, count))


def exact_right(left, right, count, left_dim=1, right_dim=0):
    return sum(product(piece, right, left_dim, right_dim) for piece in pieces_of(left, count))


def split_product(left, right, left_dim=1, right_dim=0):
    left_high, left_rest = pieces_of(left, 2)
    right_high, right_rest = pieces_of(right, 2)
    return (
        product(left_high, right_high, left_dim, right_dim)
        + product(left_high, right_rest, left_dim, right_dim)
        + product(left_rest, right_high, left_dim, right_dim)
    )


def ones_where(condition):
    return jnp.where(condition, 1.0, 0.0).astype(jnp.bfloat16)


def span_index(length):
    row = lax.broadcasted_iota(jnp.int32, (length, length), 0)
    column = lax.broadcasted_iota(jnp.int32, (length, length), 1)
    return row, column


def head_map(heads, width):
    head = lax.broadcasted_iota(jnp.int32, (heads, width), 0)
    lane = lax.broadcasted_iota(jnp.int32, (heads, width), 1)
    return ones_where(lane // (width // heads) == head)


def decays(row, column, steps, rate, seg, seg_before):
    length = steps.shape[0]
    running = exact_left(ones_where(row >= column), steps * rate, 3)
    entry = jnp.where(seg == seg_before[0:1], jnp.exp(running), 0.0)
    to_end = jnp.where(
        seg == seg[length - 1 : length], jnp.exp(running[length - 1 : length] - running), 0.0
    )
    return running, entry, to_end


def state_kernel(values, writes, steps, rate, seg, seg_before, state):
    length, width = values.shape
    heads = steps.shape[1]

    @pl.when(pl.program_id(0) == 0)
    def _():
        state[...] = jnp.zeros_like(state)

    row, column = span_index(length)
    expand = head_map(heads, width)
    step = steps[...]
    _, entry, to_end = decays(row, column, step, rate[...], seg[...], seg_before[...])
    weighted = exact_right(to_end * step, expand, 3) * values[...]
    kept = exact_right(jnp.broadcast_to(entry[length - 1 :], (8, heads)), expand, 3)[0:1]
    state[...] = kept * state[...] + exact_left(writes[...], weighted, 2, 0, 0)


def forward_kernel(
    values, writes, reads, steps, steps_row, rate, rate_row, seg, seg_row, seg_before, seg_group,
    skip, state_in, mixed, states, entries, state, total,
):
    length, width = values.shape
    heads = steps.shape[1]
    pair = 2 * (width // heads)

    @pl.when(pl.program_id(0) == 0)
    def _():
        state[...] = state_in[...]
        total[...] = jnp.zeros_like(total)

    row, column = span_index(length)
    expand = head_map(heads, width)
    step = steps[...]
    step_row = steps_row[...]
    running, entry, to_end = decays(row, column, step, rate[...], seg[...], seg_before[...])
    running_row = exact_right(step_row * rate_row[...], ones_where(row <= column), 3)
    same = (seg[...] == seg_row[...]) & (row >= column)
    scores = product(reads[...], writes[...], 1, 1)
    before = state[...]
    states[0] = before
    outer = exact_right(entry, expand, 3) * exact_left(reads[...], before, 2)
    lane = lax.broadcasted_iota(jnp.int32, (length, pair), 1)
    for j in range(heads // 2):
        lanes = slice(j * pair, (j + 1) * pair)
        value = values[:, lanes]
        mixing = []
        for h in (2 * j, 2 * j + 1):
            gap = running[:, h : h + 1] - running_row[h : h + 1, :]
            mixing.append(
                jnp.exp(jnp.where(same, gap, -1e30)) * scores * step_row[h : h + 1, :]
            )
        stacked = jnp.concatenate(
            [jnp.where(lane < pair // 2, value, 0.0), jnp.where(lane >= pair // 2, value, 0.0)],
            axis=0,
        )
        mixed[:, lanes] = (
            split_product(jnp.concatenate(mixing, axis=1), stacked)
            + outer[:, lanes]
            + skip[:, lanes] * value
        )
    weighted = exact_right(to_end * step, expand, 3) * values[...]
    kept = exact_right(jnp.broadcast_to(entry[length - 1 :], (8, heads)), expand, 3)[0:1]
    state[...] = kept * before + exact_left(writes[...], weighted, 2, 0, 0)
    whole = total[...] + running
    total[...] = whole[length - 1 :]
    entries[...] = exact_right(
        jnp.where(seg[...] == seg_group[...], jnp.exp(whole), 0.0), expand, 3
    )


def backward_kernel(
    values, grads, writes, reads, steps, steps_row, rate, rate_row, seg, seg_row, seg_before,
    skip, states, adjoint_in, values_grad, writes_grad, reads_grad, steps_grad, decay_grad,
    skip_grad, adjoint,
):
    length, width = values.shape
    heads = steps.shape[1]
    pair = 2 * (width // heads)

    @pl.when(pl.program_id(0) == 0)
    def _():
        adjoint[...] = adjoint_in[...]
        decay_grad[...] = jnp.zeros_like(decay_grad)
        skip_grad[...] = jnp.zeros_like(skip_grad)

    row, column = span_index(length)
    expand = head_map(heads, width)
    step = steps[...]
    running, entry, to_end = decays(row, column, step, rate[...], seg[...], seg_before[...])
    running_row = exact_right(steps_row[...] * rate_row[...], ones_where(row <= column), 3)
    same = (seg[...] == seg_row[...]) & (row <= column)
    write = writes[...]
    read = reads[...]
    scores = product(write, read, 1, 1)
    later = adjoint[...]
    before = states[0]
    grad = grads[...]
    value = values[...]
    weight = to_end * step
    weights = exact_right(weight, expand, 3)
    entered = exact_right(entry, expand, 3) * grad
    arriving = exact_left(write, later, 2)
    scores_grad = jnp.zeros((length, length), jnp.float32)
    lane = lax.broadcasted_iota(jnp.int32, (length, pair), 1)
    head_lane = lax.broadcasted_iota(jnp.int32, (length, heads), 1)
    source_sums = jnp.zeros((length, heads), jnp.float32)
    target_sums = []
    for j in range(heads // 2):
        lanes = slice(j * pair, (j + 1) * pair)
        grad_pair = grads[:, lanes]
        value_pair = values[:, lanes]
        mixing = []
        halves = []
        for h in (2 * j, 2 * j + 1):
            mine = (lane < pair // 2) if h % 2 == 0 else (lane >= pair // 2)
            decay = jnp.exp(jnp.where(same, running_row[h : h + 1, :] - running[:, h : h + 1], -1e30))
            stepped = decay * step[:, h : h + 1]
            mixing.append(stepped * scores)
            mixing_grad = split_product(jnp.where(mine, value_pair, 0.0), grad_pair, 1, 1)
            stepped_grad = mixing_grad * stepped
            scores_grad = scores_grad + stepped_grad
            source = jnp.sum(mixing_grad * (decay * scores), axis=1, keepdims=True)
            source_sums = jnp.where(head_lane == h, source, source_sums)
            target_sums.append(jnp.sum(stepped_grad * scores, axis=0, keepdims=True))
            halves.append(jnp.where(mine, grad_pair, 0.0))
        values_grad[:, lanes] = (
            split_product(jnp.concatenate(mixing, axis=1), jnp.concatenate(halves, axis=0))
            + weights[:, lanes] * arriving[:, lanes]
            + skip[:, lanes] * grad_pair
        )
    target_rows = jnp.concatenate(target_sums, axis=0)
    targets = exact_left(ones_where(row == column), target_rows, 3, 1, 1)
    writes_grad[...] = exact_right(scores_grad, read, 2) + split_product(
        weights * value, later, 1, 1
    )
    reads_grad[...] = exact_right(scores_grad, write, 2, 0, 0) + split_product(
        entered, before, 1, 1
    )
    inter = exact_right(entered * exact_left(read, before, 2), expand, 3, 1, 1)
    carried = exact_right(value * arriving, expand, 3, 1, 1)
    running_grad = targets + inter - source_sums * step - carried * weight
    state_sum = jnp.sum(later * before, axis=0, keepdims=True)
    state_heads = exact_right(jnp.broadcast_to(state_sum, (8, width)), expand, 3, 1, 1)[0:1]
    last = jnp.sum(carried * weight, axis=0, keepdims=True) + entry[length - 1 :] * state_heads
    logs_grad = exact_left(ones_where(row <= column), running_grad, 3) + last
    steps_grad[...] = source_sums + carried * to_end + logs_grad * rate[...]
    decay_grad[...] += jnp.sum(logs_grad * step * rate[...], axis=0, keepdims=True)
    skip_grad[...] += jnp.sum(grad * value, axis=0, keepdims=True)
    kept = exact_right(jnp.broadcast_to(entry[length - 1 :], (8, heads)), expand, 3)[0:1]
    adjoint[...] = kept * later + exact_left(read, entered, 2, 0, 0)


def scan_call(kernel, turns, reverse, operands, results, scratch, flops):
    def spec(shape, kind):
        def place(i):
            return turns - 1 - i if reverse else i

        if kind == "rows":
            return pl.BlockSpec((shape[0] // turns,) + shape[1:], lambda i: (place(i), 0))
        if kind == "columns":
            return pl.BlockSpec((shape[0], shape[1] // turns), lambda i: (0, place(i)))
        if kind == "turn":
            return pl.BlockSpec((1,) + shape[1:], lambda i: (place(i), 0, 0))
        return pl.BlockSpec(shape, lambda i: (0, 0))

    moved = sum(a.size * a.dtype.itemsize for a, _ in operands)
    return pl.pallas_call(
        kernel,
        grid=(turns,),
        in_specs=[spec(a.shape, kind) for a, kind in operands],
        out_specs=[spec(shape, kind) for shape, kind in results],
        out_shape=[jax.ShapeDtypeStruct(shape, jnp.float32) for shape, _ in results],
        scratch_shapes=[pltpu.VMEM(shape, jnp.float32) for shape in scratch],
        compiler_params=pltpu.CompilerParams(vmem_limit_bytes=40 * 1024 * 1024),
        cost_estimate=pl.CostEstimate(flops=flops, bytes_accessed=2 * moved, transcendentals=0),
    )(*[a for a, _ in operands])


def exchange_sum(blocks, axis):
    count = lax.axis_size(axis)
    place = lax.axis_index(axis)
    total = lax.dynamic_index_in_dim(blocks, place, 0, False).astype(jnp.float32)
    for hop in range(1, count):
        sent = lax.dynamic_index_in_dim(blocks, (place + hop) % count, 0, False)
        arrived = lax.ppermute(sent, axis, [(i, (i + hop) % count) for i in range(count)])
        total = total + arrived.astype(jnp.float32)
    return total


def exchange_rows(partial_sum, axis):
    count = lax.axis_size(axis)
    blocks = partial_sum.reshape((count, partial_sum.shape[0] // count) + partial_sum.shape[1:])
    return exchange_sum(blocks, axis)


def conv_apply(conv_in, rim, kernel, offset, valid):
    padded = jnp.concatenate([rim, conv_in], axis=0)
    group_rows = conv_in.shape[0]
    width = kernel.shape[0]
    total = offset[None, :]
    for tap_index in range(width):
        begin = width - 1 - tap_index
        total = total + kernel[tap_index][None, :] * jnp.where(
            valid[tap_index][:, None], padded[begin : begin + group_rows], 0.0
        )
    return jax.nn.silu(total)


def contract_last(left, right):
    return lax.dot_general(
        left, right, (((1,), (1,)), ((), ())), preferred_element_type=jnp.float32
    )


def contract_first(left, right):
    return lax.dot_general(
        left, right, (((0,), (0,)), ((), ())), preferred_element_type=jnp.float32
    )


def body(
    hidden_in,
    out_grad,
    seg_ids,
    norm_gain,
    gate_weight,
    value_weight,
    write_weight,
    read_weight,
    step_weight,
    step_bias,
    decay_log,
    skip_gain,
    conv_value,
    conv_write_read,
    conv_value_bias,
    conv_write_read_bias,
    gate_gain,
    out_weight,
):
    tensor_count = lax.axis_size("tensor")
    tensor_rank = lax.axis_index("tensor")
    data_rank = lax.axis_index("dp")
    own_rows = hidden_in.shape[0]
    group_rows = own_rows * tensor_count
    kernel_width = conv_value.shape[0]
    heads_here = step_weight.shape[1]
    inner_here = value_weight.shape[1]
    head_size = inner_here // heads_here
    state_here = write_weight.shape[1]
    state_size = state_here * tensor_count
    inner_total = inner_here * tensor_count
    gate_full, value_full, write_full, read_full, step_full, out_full = (
        lax.all_gather(gate_weight, "dp", axis=0, tiled=True),
        lax.all_gather(value_weight, "dp", axis=0, tiled=True),
        lax.all_gather(write_weight, "dp", axis=0, tiled=True),
        lax.all_gather(read_weight, "dp", axis=0, tiled=True),
        lax.all_gather(step_weight, "dp", axis=0, tiled=True),
        lax.all_gather(out_weight, "dp", axis=0, tiled=True),
    )
    hidden_rows, grad_rows = (
        lax.all_gather(hidden_in, "tensor", axis=0, tiled=True),
        lax.all_gather(out_grad, "tensor", axis=0, tiled=True),
    )
    hidden_float = hidden_rows.astype(jnp.float32)
    scale = lax.rsqrt(jnp.mean(hidden_float * hidden_float, axis=1, keepdims=True) + epsilon)
    normed = hidden_float * scale
    features = (normed * norm_gain[None, :]).astype(jnp.bfloat16)
    conv_full = jnp.concatenate([value_full, write_full, read_full], axis=1)
    gate_in = jnp.dot(features, gate_full, preferred_element_type=jnp.float32)
    conv_in = jnp.dot(features, conv_full, preferred_element_type=jnp.float32)
    step_in = jnp.dot(features, step_full, preferred_element_type=jnp.float32)
    rim = from_behind(conv_in[group_rows - (kernel_width - 1) :], "dp", 1)
    kernel = jnp.concatenate([conv_value, conv_write_read[0], conv_write_read[1]], axis=1)
    offset = jnp.concatenate([conv_value_bias, conv_write_read_bias[0], conv_write_read_bias[1]])
    padded_seg = jnp.concatenate([jnp.full((kernel_width - 1,), -1, jnp.int32), seg_ids])
    window = lax.dynamic_slice_in_dim(
        padded_seg, data_rank * group_rows, group_rows + kernel_width - 1
    )
    segment = window[kernel_width - 1 :]
    valid = jnp.stack(
        [
            window[kernel_width - 1 - tap_index : kernel_width - 1 - tap_index + group_rows]
            == segment
            for tap_index in range(kernel_width)
        ]
    )
    acted, conv_back = jax.vjp(partial(conv_apply, valid=valid), conv_in, rim, kernel, offset)
    values = acted[:, :inner_here]
    writes_low = acted[:, inner_here : inner_here + state_here].astype(jnp.bfloat16)
    reads_low = acted[:, inner_here + state_here :].astype(jnp.bfloat16)
    writes_all, reads_all = (
        lax.all_gather(writes_low, "tensor", axis=1, tiled=True),
        lax.all_gather(reads_low, "tensor", axis=1, tiled=True),
    )
    steps = jax.nn.softplus(step_in + step_bias[None, :])
    rate = -jnp.exp(decay_log)
    turns = group_rows // SPAN
    steps_row = steps.T
    rates = (rate[None, :], "whole"), (rate[:, None], "whole")
    seg_column = (segment[:, None], "rows")
    seg_line = (segment[None, :], "columns")
    before = window[kernel_width - 2 : kernel_width - 2 + group_rows][:, None]
    skip = (jnp.repeat(skip_gain, head_size)[None, :], "whole")
    state_shape = (state_size, inner_here)
    (state_end,) = scan_call(
        state_kernel,
        turns,
        False,
        [
            (values, "rows"),
            (writes_all, "rows"),
            (steps, "rows"),
            rates[0],
            seg_column,
            (before, "rows"),
        ],
        [(state_shape, "whole")],
        [],
        10**9,
    )
    state_in = from_behind(state_end, "dp", 1)
    shared = [
        (writes_all, "rows"),
        (reads_all, "rows"),
        (steps, "rows"),
        (steps_row, "columns"),
        *rates,
        seg_column,
        seg_line,
        (before, "rows"),
    ]
    mixed, states, entries = scan_call(
        forward_kernel,
        turns,
        False,
        [(values, "rows"), *shared, (before[:1], "whole"), skip, (state_in, "whole")],
        [
            (values.shape, "rows"),
            ((turns,) + state_shape, "turn"),
            (values.shape, "rows"),
        ],
        [state_shape, (1, heads_here)],
        10**10,
    )
    gate_act = jax.nn.silu(gate_in)
    gated = mixed * gate_act
    branch_grad = jnp.dot(grad_rows, out_full, preferred_element_type=jnp.float32)
    scaled = branch_grad * gate_gain[None, :]
    squares, dots = lax.psum(
        jnp.stack([jnp.sum(gated * gated, axis=1), jnp.sum(scaled * gated, axis=1)]), "tensor"
    )
    rms = lax.rsqrt(squares / inner_total + epsilon)
    branch = (gated * rms[:, None] * gate_gain[None, :]).astype(jnp.bfloat16)
    summed = exchange_rows(contract_last(branch, out_full).astype(jnp.bfloat16), "tensor")
    layer_out = hidden_in.astype(jnp.float32) + summed
    out_weight_grad = exchange_rows(contract_first(grad_rows, branch).astype(jnp.bfloat16), "dp")
    gate_gain_grad = jnp.sum(branch_grad * gated * rms[:, None], axis=0)
    gated_grad = rms[:, None] * scaled - gated * (rms * rms * rms * dots / inner_total)[:, None]
    mixed_grad = gated_grad * gate_act
    gate_sigmoid = jax.nn.sigmoid(gate_in)
    gate_grad = gated_grad * mixed * gate_sigmoid * (1.0 + gate_in * (1.0 - gate_sigmoid))
    carry_term = lax.dot_general(
        reads_all.astype(jnp.float32),
        entries * mixed_grad,
        (((0,), (0,)), ((), ())),
        precision=highest,
    )
    adjoint_in = from_behind(carry_term, "dp", -1)
    values_grad, writes_grad, reads_grad, steps_grad, decay_log_grad, skip_grad = scan_call(
        backward_kernel,
        turns,
        True,
        [
            (values, "rows"),
            (mixed_grad, "rows"),
            *shared,
            skip,
            (states, "turn"),
            (adjoint_in, "whole"),
        ],
        [
            (values.shape, "rows"),
            (writes_all.shape, "rows"),
            (writes_all.shape, "rows"),
            (steps.shape, "rows"),
            ((1, heads_here), "whole"),
            ((1, inner_here), "whole"),
        ],
        [state_shape],
        2 * 10**10,
    )
    decay_log_grad = decay_log_grad[0]
    skip_grad = jnp.sum(skip_grad.reshape(heads_here, head_size), axis=1)
    both = jnp.stack([writes_grad, reads_grad], axis=1).reshape(
        group_rows, 2, tensor_count, state_here
    )
    both = both.transpose(2, 0, 1, 3).reshape(tensor_count, group_rows, 2 * state_here)
    pair_part = exchange_sum(both, "tensor")
    acted_grad = jnp.concatenate([values_grad, pair_part], axis=1)
    conv_in_grad, rim_grad, kernel_grad, offset_grad = conv_back(acted_grad)
    rim_return = from_behind(rim_grad, "dp", -1)
    edge = group_rows - (kernel_width - 1)
    conv_in_grad = jnp.concatenate([conv_in_grad[:edge], conv_in_grad[edge:] + rim_return], axis=0)
    step_pre = steps_grad * jax.nn.sigmoid(step_in + step_bias[None, :])
    step_bias_grad = jnp.sum(step_pre, axis=0)
    gate_low = gate_grad.astype(jnp.bfloat16)
    conv_low = conv_in_grad.astype(jnp.bfloat16)
    step_low = step_pre.astype(jnp.bfloat16)
    features_grad = (
        contract_last(gate_low, gate_full)
        + contract_last(conv_low, conv_full)
        + contract_last(step_low, step_full)
    )
    gain_part = jnp.sum(features_grad * normed, axis=0)
    own_features_grad = exchange_rows(features_grad.astype(jnp.bfloat16), "tensor")
    norm_gain_grad = lax.psum_scatter(gain_part, "tensor", scatter_dimension=0, tiled=True)
    own_normed = lax.dynamic_slice_in_dim(normed, tensor_rank * own_rows, own_rows, 0)
    own_scale = lax.dynamic_slice_in_dim(scale, tensor_rank * own_rows, own_rows, 0)
    normed_grad = own_features_grad * norm_gain[None, :]
    input_grad = out_grad.astype(jnp.float32) + own_scale * (
        normed_grad - own_normed * jnp.mean(normed_grad * own_normed, axis=1, keepdims=True)
    )
    lows = jnp.concatenate([gate_low, conv_low, step_low], axis=1)
    joint = exchange_rows(contract_first(features, lows).astype(jnp.bfloat16), "dp")
    cuts = (inner_here, 2 * inner_here, 2 * inner_here + state_here, 2 * (inner_here + state_here))
    weight_sums = (*jnp.split(joint, cuts, axis=1), out_weight_grad)
    conv_value_grad = kernel_grad[:, :inner_here]
    conv_pair_grad = jnp.stack(
        [
            kernel_grad[:, inner_here : inner_here + state_here],
            kernel_grad[:, inner_here + state_here :],
        ]
    )
    conv_value_bias_grad = offset_grad[:inner_here]
    conv_pair_bias_grad = jnp.stack(
        [offset_grad[inner_here : inner_here + state_here], offset_grad[inner_here + state_here :]]
    )
    small = (
        norm_gain_grad,
        gate_gain_grad,
        step_bias_grad,
        decay_log_grad,
        skip_grad,
        conv_value_grad,
        conv_pair_grad,
        conv_value_bias_grad,
        conv_pair_bias_grad,
    )
    packed = lax.psum(jnp.concatenate([item.reshape(-1) for item in small]), "dp")
    small_sums = []
    begin = 0
    for item in small:
        small_sums.append(packed[begin : begin + item.size].reshape(item.shape))
        begin += item.size
    return (
        layer_out,
        input_grad,
        small_sums[0],
        weight_sums[0],
        weight_sums[1],
        weight_sums[2],
        weight_sums[3],
        weight_sums[4],
        small_sums[2],
        small_sums[3],
        small_sums[4],
        small_sums[5],
        small_sums[6],
        small_sums[7],
        small_sums[8],
        small_sums[1],
        weight_sums[5],
    )


def solution(mesh):
    return jax.shard_map(
        body,
        mesh=mesh,
        in_specs=(
            P(("dp", "tensor"), None),
            P(("dp", "tensor"), None),
            P(),
            P(),
            P("dp", "tensor"),
            P("dp", "tensor"),
            P("dp", "tensor"),
            P("dp", "tensor"),
            P("dp", "tensor"),
            P("tensor"),
            P("tensor"),
            P("tensor"),
            P(None, "tensor"),
            P(None, None, "tensor"),
            P("tensor"),
            P(None, "tensor"),
            P("tensor"),
            P("dp", "tensor"),
        ),
        out_specs=(
            P(("dp", "tensor"), None),
            P(("dp", "tensor"), None),
            P("tensor"),
            P("dp", "tensor"),
            P("dp", "tensor"),
            P("dp", "tensor"),
            P("dp", "tensor"),
            P("dp", "tensor"),
            P("tensor"),
            P("tensor"),
            P("tensor"),
            P(None, "tensor"),
            P(None, None, "tensor"),
            P("tensor"),
            P(None, "tensor"),
            P("tensor"),
            P("dp", "tensor"),
        ),
        check_vma=False,
    )
```

```python
from functools import partial

import jax
import jax.numpy as jnp
from jax import lax
from jax.experimental import pallas as pl
from jax.experimental.pallas import tpu as pltpu
from jax.sharding import PartitionSpec as P

SPAN = 128


epsilon = 1e-05
highest = lax.Precision.HIGHEST


def from_behind(value, axis, steps):
    count = lax.axis_size(axis)
    leading, last = (max(0, -steps), min(count, count - steps))
    return lax.ppermute(value, axis, [(source, source + steps) for source in range(leading, last)])


def product(left, right, left_dim=1, right_dim=0):
    return lax.dot_general(
        left, right, (((left_dim,), (right_dim,)), ((), ())), preferred_element_type=jnp.float32
    )


def pieces_of(value, count):
    pieces = []
    for _ in range(count - 1):
        piece = value.astype(jnp.bfloat16)
        pieces.append(piece)
        value = value - piece.astype(jnp.float32)
    return pieces + [value.astype(jnp.bfloat16)]


def exact_left(left, right, count, left_dim=1, right_dim=0):
    return sum(product(left, piece, left_dim, right_dim) for piece in pieces_of(right, count))


def exact_right(left, right, count, left_dim=1, right_dim=0):
    return sum(product(piece, right, left_dim, right_dim) for piece in pieces_of(left, count))


def split_product(left, right, left_dim=1, right_dim=0):
    left_high, left_rest = pieces_of(left, 2)
    right_high, right_rest = pieces_of(right, 2)
    return (
        product(left_high, right_high, left_dim, right_dim)
        + product(left_high, right_rest, left_dim, right_dim)
        + product(left_rest, right_high, left_dim, right_dim)
    )


def ones_where(condition):
    return jnp.where(condition, 1.0, 0.0).astype(jnp.bfloat16)


def span_index(length):
    row = lax.broadcasted_iota(jnp.int32, (length, length), 0)
    column = lax.broadcasted_iota(jnp.int32, (length, length), 1)
    return row, column


def head_map(heads, width):
    head = lax.broadcasted_iota(jnp.int32, (heads, width), 0)
    lane = lax.broadcasted_iota(jnp.int32, (heads, width), 1)
    return ones_where(lane // (width // heads) == head)


def decays(row, column, steps, rate, seg, seg_before):
    length = steps.shape[0]
    running = exact_left(ones_where(row >= column), steps * rate, 3)
    entry = jnp.where(seg == seg_before[0:1], jnp.exp(running), 0.0)
    to_end = jnp.where(
        seg == seg[length - 1 : length], jnp.exp(running[length - 1 : length] - running), 0.0
    )
    return running, entry, to_end


def joined(pairs, second):
    count, _, width = pairs.shape
    begin = width // 2 if second else 0
    return jnp.concatenate(
        [pairs[i, :, begin : begin + width // 2] for i in range(count)], axis=1
    )


def state_kernel(values, pairs, steps, rate, seg, seg_before, state):
    length, width = values.shape
    heads = steps.shape[1]

    @pl.when(pl.program_id(0) == 0)
    def _():
        state[...] = jnp.zeros_like(state)

    row, column = span_index(length)
    expand = head_map(heads, width)
    step = steps[...]
    _, entry, to_end = decays(row, column, step, rate[...], seg[...], seg_before[...])
    weighted = exact_right(to_end * step, expand, 3) * values[...]
    kept = exact_right(jnp.broadcast_to(entry[length - 1 :], (8, heads)), expand, 3)[0:1]
    state[...] = kept * state[...] + exact_left(joined(pairs, False), weighted, 2, 0, 0)


def forward_kernel(
    values, pairs, steps, steps_row, rate, rate_row, seg, seg_row, seg_before, seg_group,
    skip, state_in, mixed, states, entries, state, total,
):
    length, width = values.shape
    heads = steps.shape[1]
    pair = 2 * (width // heads)

    @pl.when(pl.program_id(0) == 0)
    def _():
        state[...] = state_in[...]
        total[...] = jnp.zeros_like(total)

    row, column = span_index(length)
    expand = head_map(heads, width)
    step = steps[...]
    step_row = steps_row[...]
    running, entry, to_end = decays(row, column, step, rate[...], seg[...], seg_before[...])
    running_row = exact_right(step_row * rate_row[...], ones_where(row <= column), 3)
    same = (seg[...] == seg_row[...]) & (row >= column)
    write, read = joined(pairs, False), joined(pairs, True)
    scores = product(read, write, 1, 1)
    before = state[...]
    states[0] = before
    outer = exact_right(entry, expand, 3) * exact_left(read, before, 2)
    lane = lax.broadcasted_iota(jnp.int32, (length, pair), 1)
    for j in range(heads // 2):
        lanes = slice(j * pair, (j + 1) * pair)
        value = values[:, lanes]
        mixing = []
        for h in (2 * j, 2 * j + 1):
            gap = running[:, h : h + 1] - running_row[h : h + 1, :]
            mixing.append(
                jnp.exp(jnp.where(same, gap, -1e30)) * scores * step_row[h : h + 1, :]
            )
        stacked = jnp.concatenate(
            [jnp.where(lane < pair // 2, value, 0.0), jnp.where(lane >= pair // 2, value, 0.0)],
            axis=0,
        )
        mixed[:, lanes] = (
            split_product(jnp.concatenate(mixing, axis=1), stacked)
            + outer[:, lanes]
            + skip[:, lanes] * value
        )
    weighted = exact_right(to_end * step, expand, 3) * values[...]
    kept = exact_right(jnp.broadcast_to(entry[length - 1 :], (8, heads)), expand, 3)[0:1]
    state[...] = kept * before + exact_left(write, weighted, 2, 0, 0)
    whole = total[...] + running
    total[...] = whole[length - 1 :]
    entries[...] = exact_right(
        jnp.where(seg[...] == seg_group[...], jnp.exp(whole), 0.0), expand, 3
    )


def backward_kernel(
    values, grads, pairs, steps, steps_row, rate, rate_row, seg, seg_row, seg_before,
    skip, states, adjoint_in, values_grad, pairs_grad, steps_grad, decay_grad,
    skip_grad, adjoint,
):
    length, width = values.shape
    heads = steps.shape[1]
    pair = 2 * (width // heads)

    @pl.when(pl.program_id(0) == 0)
    def _():
        adjoint[...] = adjoint_in[...]
        decay_grad[...] = jnp.zeros_like(decay_grad)
        skip_grad[...] = jnp.zeros_like(skip_grad)

    row, column = span_index(length)
    expand = head_map(heads, width)
    step = steps[...]
    running, entry, to_end = decays(row, column, step, rate[...], seg[...], seg_before[...])
    running_row = exact_right(steps_row[...] * rate_row[...], ones_where(row <= column), 3)
    same = (seg[...] == seg_row[...]) & (row <= column)
    write, read = joined(pairs, False), joined(pairs, True)
    scores = product(write, read, 1, 1)
    later = adjoint[...]
    before = states[0]
    grad = grads[...]
    value = values[...]
    weight = to_end * step
    weights = exact_right(weight, expand, 3)
    entered = exact_right(entry, expand, 3) * grad
    arriving = exact_left(write, later, 2)
    scores_grad = jnp.zeros((length, length), jnp.float32)
    lane = lax.broadcasted_iota(jnp.int32, (length, pair), 1)
    head_lane = lax.broadcasted_iota(jnp.int32, (length, heads), 1)
    source_sums = jnp.zeros((length, heads), jnp.float32)
    target_sums = []
    for j in range(heads // 2):
        lanes = slice(j * pair, (j + 1) * pair)
        grad_pair = grads[:, lanes]
        value_pair = values[:, lanes]
        mixing = []
        halves = []
        for h in (2 * j, 2 * j + 1):
            mine = (lane < pair // 2) if h % 2 == 0 else (lane >= pair // 2)
            decay = jnp.exp(jnp.where(same, running_row[h : h + 1, :] - running[:, h : h + 1], -1e30))
            stepped = decay * step[:, h : h + 1]
            mixing.append(stepped * scores)
            mixing_grad = split_product(jnp.where(mine, value_pair, 0.0), grad_pair, 1, 1)
            stepped_grad = mixing_grad * stepped
            scores_grad = scores_grad + stepped_grad
            source = jnp.sum(mixing_grad * (decay * scores), axis=1, keepdims=True)
            source_sums = jnp.where(head_lane == h, source, source_sums)
            target_sums.append(jnp.sum(stepped_grad * scores, axis=0, keepdims=True))
            halves.append(jnp.where(mine, grad_pair, 0.0))
        values_grad[:, lanes] = (
            split_product(jnp.concatenate(mixing, axis=1), jnp.concatenate(halves, axis=0))
            + weights[:, lanes] * arriving[:, lanes]
            + skip[:, lanes] * grad_pair
        )
    target_rows = jnp.concatenate(target_sums, axis=0)
    targets = exact_left(ones_where(row == column), target_rows, 3, 1, 1)
    writes_grad = exact_right(scores_grad, read, 2) + split_product(
        weights * value, later, 1, 1
    )
    reads_grad = exact_right(scores_grad, write, 2, 0, 0) + split_product(
        entered, before, 1, 1
    )
    share = pairs.shape[2] // 2
    for i in range(pairs.shape[0]):
        mine = slice(i * share, (i + 1) * share)
        pairs_grad[i] = jnp.concatenate([writes_grad[:, mine], reads_grad[:, mine]], axis=1)
    inter = exact_right(entered * exact_left(read, before, 2), expand, 3, 1, 1)
    carried = exact_right(value * arriving, expand, 3, 1, 1)
    running_grad = targets + inter - source_sums * step - carried * weight
    state_sum = jnp.sum(later * before, axis=0, keepdims=True)
    state_heads = exact_right(jnp.broadcast_to(state_sum, (8, width)), expand, 3, 1, 1)[0:1]
    last = jnp.sum(carried * weight, axis=0, keepdims=True) + entry[length - 1 :] * state_heads
    logs_grad = exact_left(ones_where(row <= column), running_grad, 3) + last
    steps_grad[...] = source_sums + carried * to_end + logs_grad * rate[...]
    decay_grad[...] += jnp.sum(logs_grad * step * rate[...], axis=0, keepdims=True)
    skip_grad[...] += jnp.sum(grad * value, axis=0, keepdims=True)
    kept = exact_right(jnp.broadcast_to(entry[length - 1 :], (8, heads)), expand, 3)[0:1]
    adjoint[...] = kept * later + exact_left(read, entered, 2, 0, 0)


def scan_call(kernel, turns, reverse, operands, results, scratch, flops):
    def spec(shape, kind):
        def place(i):
            return turns - 1 - i if reverse else i

        if kind == "rows":
            return pl.BlockSpec((shape[0] // turns,) + shape[1:], lambda i: (place(i), 0))
        if kind == "columns":
            return pl.BlockSpec((shape[0], shape[1] // turns), lambda i: (0, place(i)))
        if kind == "parts":
            return pl.BlockSpec(
                (shape[0], shape[1] // turns, shape[2]), lambda i: (0, place(i), 0)
            )
        if kind == "turn":
            return pl.BlockSpec((1,) + shape[1:], lambda i: (place(i), 0, 0))
        return pl.BlockSpec(shape, lambda i: (0, 0))

    moved = sum(a.size * a.dtype.itemsize for a, _ in operands)
    return pl.pallas_call(
        kernel,
        grid=(turns,),
        in_specs=[spec(a.shape, kind) for a, kind in operands],
        out_specs=[spec(shape, kind) for shape, kind in results],
        out_shape=[jax.ShapeDtypeStruct(shape, jnp.float32) for shape, _ in results],
        scratch_shapes=[pltpu.VMEM(shape, jnp.float32) for shape in scratch],
        compiler_params=pltpu.CompilerParams(vmem_limit_bytes=40 * 1024 * 1024),
        cost_estimate=pl.CostEstimate(flops=flops, bytes_accessed=2 * moved, transcendentals=0),
    )(*[a for a, _ in operands])


def exchange_sum(blocks, axis):
    count = lax.axis_size(axis)
    place = lax.axis_index(axis)
    total = lax.dynamic_index_in_dim(blocks, place, 0, False).astype(jnp.float32)
    for hop in range(1, count):
        sent = lax.dynamic_index_in_dim(blocks, (place + hop) % count, 0, False)
        arrived = lax.ppermute(sent, axis, [(i, (i + hop) % count) for i in range(count)])
        total = total + arrived.astype(jnp.float32)
    return total


def exchange_rows(partial_sum, axis):
    count = lax.axis_size(axis)
    blocks = partial_sum.reshape((count, partial_sum.shape[0] // count) + partial_sum.shape[1:])
    return exchange_sum(blocks, axis)


def transfer_kernel(plan, *refs):
    count = len(plan)
    sources, targets = refs[:count], refs[count : 2 * count]
    send, receive, local = refs[2 * count :]
    axes = sorted({axis for axis, _ in plan})
    barrier = pltpu.get_barrier_semaphore()
    for axis in axes:
        size = lax.axis_size(axis)
        for hop in range(1, size):
            peer = lax.rem(lax.axis_index(axis) + hop, size)
            pl.semaphore_signal(
                barrier, inc=1, device_id={axis: peer}, device_id_type=pl.DeviceIdType.MESH
            )
    pl.semaphore_wait(barrier, sum(lax.axis_size(axis) - 1 for axis in axes))
    copies = []
    slot = 0
    for item, (axis, blocks) in enumerate(plan):
        size = lax.axis_size(axis)
        me = lax.axis_index(axis)
        for hop in range(1, size):
            peer = lax.rem(me + hop, size)
            copy = pltpu.make_async_remote_copy(
                src_ref=sources[item].at[peer] if blocks else sources[item],
                dst_ref=targets[item].at[me],
                send_sem=send.at[slot],
                recv_sem=receive.at[slot],
                device_id={axis: peer},
                device_id_type=pl.DeviceIdType.MESH,
            )
            copy.start()
            copies.append(copy)
            slot += 1
        own = pltpu.make_async_copy(
            sources[item].at[me] if blocks else sources[item], targets[item].at[me], local.at[item]
        )
        own.start()
        copies.append(own)
    for copy in copies:
        copy.wait()


def transfer(items, number):
    plan = tuple((axis, blocks) for _, axis, blocks in items)
    shapes = []
    slots = 0
    for array, axis, blocks in items:
        size = lax.axis_size(axis)
        shapes.append(
            jax.ShapeDtypeStruct(array.shape if blocks else (size,) + array.shape, array.dtype)
        )
        slots += size - 1
    return pl.pallas_call(
        partial(transfer_kernel, plan),
        in_specs=[pl.BlockSpec(memory_space=pl.ANY)] * len(items),
        out_specs=[pl.BlockSpec(memory_space=pl.ANY)] * len(items),
        out_shape=shapes,
        scratch_shapes=[
            pltpu.SemaphoreType.DMA((slots,)),
            pltpu.SemaphoreType.DMA((slots,)),
            pltpu.SemaphoreType.DMA((len(items),)),
        ],
        compiler_params=pltpu.CompilerParams(collective_id=number, has_side_effects=True),
    )(*[array for array, _, _ in items])


def blocks_of(array, axis):
    count = lax.axis_size(axis)
    return array.reshape((count, array.shape[0] // count) + array.shape[1:])


def total_of(arrived):
    return jnp.sum(arrived.astype(jnp.float32), axis=0)


def conv_apply(conv_in, rim, kernel, offset, valid):
    padded = jnp.concatenate([rim, conv_in], axis=0)
    group_rows = conv_in.shape[0]
    width = kernel.shape[0]
    total = offset[None, :]
    for tap_index in range(width):
        begin = width - 1 - tap_index
        total = total + kernel[tap_index][None, :] * jnp.where(
            valid[tap_index][:, None], padded[begin : begin + group_rows], 0.0
        )
    return jax.nn.silu(total)


def contract_last(left, right):
    return lax.dot_general(
        left, right, (((1,), (1,)), ((), ())), preferred_element_type=jnp.float32
    )


def contract_first(left, right):
    return lax.dot_general(
        left, right, (((0,), (0,)), ((), ())), preferred_element_type=jnp.float32
    )


def body(
    hidden_in,
    out_grad,
    seg_ids,
    norm_gain,
    gate_weight,
    value_weight,
    write_weight,
    read_weight,
    step_weight,
    step_bias,
    decay_log,
    skip_gain,
    conv_value,
    conv_write_read,
    conv_value_bias,
    conv_write_read_bias,
    gate_gain,
    out_weight,
):
    tensor_count = lax.axis_size("tensor")
    tensor_rank = lax.axis_index("tensor")
    data_rank = lax.axis_index("dp")
    own_rows = hidden_in.shape[0]
    group_rows = own_rows * tensor_count
    kernel_width = conv_value.shape[0]
    heads_here = step_weight.shape[1]
    inner_here = value_weight.shape[1]
    head_size = inner_here // heads_here
    state_here = write_weight.shape[1]
    state_size = state_here * tensor_count
    inner_total = inner_here * tensor_count
    gate_full, value_full, rest_full, hidden_rows = transfer(
        [
            (gate_weight, "dp", False),
            (value_weight, "dp", False),
            (jnp.concatenate([write_weight, read_weight, step_weight], axis=1), "dp", False),
            (hidden_in, "tensor", False),
        ],
        1,
    )
    gate_full, value_full, rest_full, hidden_rows = (
        item.reshape((-1, item.shape[2]))
        for item in (gate_full, value_full, rest_full, hidden_rows)
    )
    grad_source, out_source, hidden_rows = lax.optimization_barrier(
        (out_grad, out_weight, hidden_rows)
    )
    grad_rows = lax.all_gather(grad_source, "tensor", axis=0, tiled=True)
    out_full = lax.all_gather(out_source, "dp", axis=0, tiled=True)
    hidden_float = hidden_rows.astype(jnp.float32)
    scale = lax.rsqrt(jnp.mean(hidden_float * hidden_float, axis=1, keepdims=True) + epsilon)
    normed = hidden_float * scale
    features = (normed * norm_gain[None, :]).astype(jnp.bfloat16)
    gate_in = jnp.dot(features, gate_full, preferred_element_type=jnp.float32)
    value_in = jnp.dot(features, value_full, preferred_element_type=jnp.float32)
    rest_in = jnp.dot(features, rest_full, preferred_element_type=jnp.float32)
    pair_in, step_in = rest_in[:, : 2 * state_here], rest_in[:, 2 * state_here :]
    rim = from_behind(
        jnp.concatenate(
            [item[group_rows - (kernel_width - 1) :] for item in (value_in, pair_in)], axis=1
        ),
        "dp",
        1,
    )
    value_rim, pair_rim = rim[:, :inner_here], rim[:, inner_here:]
    pair_kernel = jnp.concatenate([conv_write_read[0], conv_write_read[1]], axis=1)
    pair_offset = conv_write_read_bias.reshape(-1)
    padded_seg = jnp.concatenate([jnp.full((kernel_width - 1,), -1, jnp.int32), seg_ids])
    window = lax.dynamic_slice_in_dim(
        padded_seg, data_rank * group_rows, group_rows + kernel_width - 1
    )
    segment = window[kernel_width - 1 :]
    valid = jnp.stack(
        [
            window[kernel_width - 1 - tap_index : kernel_width - 1 - tap_index + group_rows]
            == segment
            for tap_index in range(kernel_width)
        ]
    )
    convolve = partial(conv_apply, valid=valid)
    pair, pair_back = jax.vjp(convolve, pair_in, pair_rim, pair_kernel, pair_offset)
    values, value_back = jax.vjp(convolve, value_in, value_rim, conv_value, conv_value_bias)
    (pairs,) = transfer([(pair.astype(jnp.bfloat16), "tensor", False)], 2)
    steps = jax.nn.softplus(step_in + step_bias[None, :])
    rate = -jnp.exp(decay_log)
    turns = group_rows // SPAN
    steps_row = steps.T
    rates = (rate[None, :], "whole"), (rate[:, None], "whole")
    seg_column = (segment[:, None], "rows")
    seg_line = (segment[None, :], "columns")
    before = window[kernel_width - 2 : kernel_width - 2 + group_rows][:, None]
    skip = (jnp.repeat(skip_gain, head_size)[None, :], "whole")
    state_shape = (state_size, inner_here)
    (state_end,) = scan_call(
        state_kernel,
        turns,
        False,
        [
            (values, "rows"),
            (pairs, "parts"),
            (steps, "rows"),
            rates[0],
            seg_column,
            (before, "rows"),
        ],
        [(state_shape, "whole")],
        [],
        10**9,
    )
    state_in = from_behind(state_end, "dp", 1)
    shared = [
        (pairs, "parts"),
        (steps, "rows"),
        (steps_row, "columns"),
        *rates,
        seg_column,
        seg_line,
        (before, "rows"),
    ]
    mixed, states, entries = scan_call(
        forward_kernel,
        turns,
        False,
        [(values, "rows"), *shared, (before[:1], "whole"), skip, (state_in, "whole")],
        [
            (values.shape, "rows"),
            ((turns,) + state_shape, "turn"),
            (values.shape, "rows"),
        ],
        [state_shape, (1, heads_here)],
        10**10,
    )
    gate_act = jax.nn.silu(gate_in)
    gated = mixed * gate_act
    branch_grad = jnp.dot(grad_rows, out_full, preferred_element_type=jnp.float32)
    scaled = branch_grad * gate_gain[None, :]
    (token_sums,) = transfer(
        [
            (
                jnp.stack([jnp.sum(gated * gated, axis=1), jnp.sum(scaled * gated, axis=1)]),
                "tensor",
                False,
            )
        ],
        3,
    )
    squares, dots = total_of(token_sums)
    rms = lax.rsqrt(squares / inner_total + epsilon)
    branch = (gated * rms[:, None] * gate_gain[None, :]).astype(jnp.bfloat16)
    summed = exchange_rows(contract_last(branch, out_full).astype(jnp.bfloat16), "tensor")
    layer_out = hidden_in.astype(jnp.float32) + summed
    out_weight_grad = exchange_rows(contract_first(grad_rows, branch).astype(jnp.bfloat16), "dp")
    gate_gain_grad = jnp.sum(branch_grad * gated * rms[:, None], axis=0)
    gated_grad = rms[:, None] * scaled - gated * (rms * rms * rms * dots / inner_total)[:, None]
    mixed_grad = gated_grad * gate_act
    gate_sigmoid = jax.nn.sigmoid(gate_in)
    gate_grad = gated_grad * mixed * gate_sigmoid * (1.0 + gate_in * (1.0 - gate_sigmoid))
    carry_term = lax.dot_general(
        pairs[:, :, state_here:].transpose(1, 0, 2).reshape(group_rows, state_size).astype(jnp.float32),
        entries * mixed_grad,
        (((0,), (0,)), ((), ())),
        precision=highest,
    )
    adjoint_in = from_behind(carry_term, "dp", -1)
    values_grad, pairs_grad, steps_grad, decay_log_grad, skip_grad = scan_call(
        backward_kernel,
        turns,
        True,
        [
            (values, "rows"),
            (mixed_grad, "rows"),
            *shared,
            skip,
            (states, "turn"),
            (adjoint_in, "whole"),
        ],
        [
            (values.shape, "rows"),
            (pairs.shape, "parts"),
            (steps.shape, "rows"),
            ((1, heads_here), "whole"),
            ((1, inner_here), "whole"),
        ],
        [state_shape],
        2 * 10**10,
    )
    decay_log_grad = decay_log_grad[0]
    skip_grad = jnp.sum(skip_grad.reshape(heads_here, head_size), axis=1)
    pair_grad = exchange_sum(pairs_grad, "tensor")
    value_in_grad, value_rim_grad, value_kernel_grad, value_offset_grad = value_back(values_grad)
    pair_in_grad, pair_rim_grad, pair_kernel_grad, pair_offset_grad = pair_back(pair_grad)
    edge = group_rows - (kernel_width - 1)
    value_in_grad = value_in_grad.at[edge:].add(from_behind(value_rim_grad, "dp", -1))
    pair_in_grad = pair_in_grad.at[edge:].add(from_behind(pair_rim_grad, "dp", -1))
    step_pre = steps_grad * jax.nn.sigmoid(step_in + step_bias[None, :])
    step_bias_grad = jnp.sum(step_pre, axis=0)
    gate_low = gate_grad.astype(jnp.bfloat16)
    value_low = value_in_grad.astype(jnp.bfloat16)
    rest_low = jnp.concatenate([pair_in_grad, step_pre], axis=1).astype(jnp.bfloat16)
    features_grad = (
        contract_last(gate_low, gate_full)
        + contract_last(value_low, value_full)
        + contract_last(rest_low, rest_full)
    )
    gain_part = jnp.sum(features_grad * normed, axis=0)
    gate_share, value_share, rest_share = (
        blocks_of(contract_first(features, low).astype(jnp.bfloat16), "dp")
        for low in (gate_low, value_low, rest_low)
    )
    small = (
        gain_part,
        gate_gain_grad,
        step_bias_grad,
        decay_log_grad,
        skip_grad,
        value_kernel_grad,
        pair_kernel_grad,
        value_offset_grad,
        pair_offset_grad,
    )
    flat = jnp.concatenate([item.reshape(-1) for item in small])
    flat = jnp.pad(flat, (0, -flat.size % 1024)).reshape(-1, 128)
    features_parts, gate_parts, value_parts, rest_parts, flat_parts = transfer(
        [
            (blocks_of(features_grad.astype(jnp.bfloat16), "tensor"), "tensor", True),
            (gate_share, "dp", True),
            (value_share, "dp", True),
            (rest_share, "dp", True),
            (flat, "dp", False),
        ],
        4,
    )
    own_features_grad = total_of(features_parts)
    packed = total_of(flat_parts).reshape(-1)
    small_sums = []
    begin = 0
    for item in small:
        small_sums.append(packed[begin : begin + item.size].reshape(item.shape))
        begin += item.size
    (gain_parts,) = transfer(
        [(small_sums[0].reshape(tensor_count, 1, -1), "tensor", True)],
        5,
    )
    norm_gain_grad = total_of(gain_parts)[0]
    own_normed = lax.dynamic_slice_in_dim(normed, tensor_rank * own_rows, own_rows, 0)
    own_scale = lax.dynamic_slice_in_dim(scale, tensor_rank * own_rows, own_rows, 0)
    normed_grad = own_features_grad * norm_gain[None, :]
    input_grad = out_grad.astype(jnp.float32) + own_scale * (
        normed_grad - own_normed * jnp.mean(normed_grad * own_normed, axis=1, keepdims=True)
    )
    rest_sum = total_of(rest_parts)
    weight_sums = (
        total_of(gate_parts),
        total_of(value_parts),
        rest_sum[:, :state_here],
        rest_sum[:, state_here : 2 * state_here],
        rest_sum[:, 2 * state_here :],
        out_weight_grad,
    )

    def paired(array):
        return jnp.stack([array[..., :state_here], array[..., state_here:]])

    return (
        layer_out,
        input_grad,
        norm_gain_grad,
        weight_sums[0],
        weight_sums[1],
        weight_sums[2],
        weight_sums[3],
        weight_sums[4],
        small_sums[2],
        small_sums[3],
        small_sums[4],
        small_sums[5],
        paired(small_sums[6]),
        small_sums[7],
        paired(small_sums[8]),
        small_sums[1],
        weight_sums[5],
    )


def solution(mesh):
    return jax.shard_map(
        body,
        mesh=mesh,
        in_specs=(
            P(("dp", "tensor"), None),
            P(("dp", "tensor"), None),
            P(),
            P(),
            P("dp", "tensor"),
            P("dp", "tensor"),
            P("dp", "tensor"),
            P("dp", "tensor"),
            P("dp", "tensor"),
            P("tensor"),
            P("tensor"),
            P("tensor"),
            P(None, "tensor"),
            P(None, None, "tensor"),
            P("tensor"),
            P(None, "tensor"),
            P("tensor"),
            P("dp", "tensor"),
        ),
        out_specs=(
            P(("dp", "tensor"), None),
            P(("dp", "tensor"), None),
            P("tensor"),
            P("dp", "tensor"),
            P("dp", "tensor"),
            P("dp", "tensor"),
            P("dp", "tensor"),
            P("dp", "tensor"),
            P("tensor"),
            P("tensor"),
            P("tensor"),
            P(None, "tensor"),
            P(None, None, "tensor"),
            P("tensor"),
            P(None, "tensor"),
            P("tensor"),
            P("dp", "tensor"),
        ),
        check_vma=False,
    )
```

```python
from functools import partial

import jax
import jax.numpy as jnp
from jax import lax
from jax.experimental import pallas as pl
from jax.experimental.pallas import tpu as pltpu
from jax.sharding import PartitionSpec as P

SPAN = 128


epsilon = 1e-05
highest = lax.Precision.HIGHEST


def from_behind(value, axis, steps):
    count = lax.axis_size(axis)
    leading, last = (max(0, -steps), min(count, count - steps))
    return lax.ppermute(value, axis, [(source, source + steps) for source in range(leading, last)])


def product(left, right, left_dim=1, right_dim=0):
    return lax.dot_general(
        left, right, (((left_dim,), (right_dim,)), ((), ())), preferred_element_type=jnp.float32
    )


def pieces_of(value, count):
    pieces = []
    for _ in range(count - 1):
        piece = value.astype(jnp.bfloat16)
        pieces.append(piece)
        value = value - piece.astype(jnp.float32)
    return pieces + [value.astype(jnp.bfloat16)]


def exact_left(left, right, count, left_dim=1, right_dim=0):
    return sum(product(left, piece, left_dim, right_dim) for piece in pieces_of(right, count))


def exact_right(left, right, count, left_dim=1, right_dim=0):
    return sum(product(piece, right, left_dim, right_dim) for piece in pieces_of(left, count))


def split_product(left, right, left_dim=1, right_dim=0):
    left_high, left_rest = pieces_of(left, 2)
    right_high, right_rest = pieces_of(right, 2)
    return (
        product(left_high, right_high, left_dim, right_dim)
        + product(left_high, right_rest, left_dim, right_dim)
        + product(left_rest, right_high, left_dim, right_dim)
    )


def ones_where(condition):
    return jnp.where(condition, 1.0, 0.0).astype(jnp.bfloat16)


def span_index(length):
    row = lax.broadcasted_iota(jnp.int32, (length, length), 0)
    column = lax.broadcasted_iota(jnp.int32, (length, length), 1)
    return row, column


def head_map(heads, width):
    head = lax.broadcasted_iota(jnp.int32, (heads, width), 0)
    lane = lax.broadcasted_iota(jnp.int32, (heads, width), 1)
    return ones_where(lane // (width // heads) == head)


def decays(row, column, steps, rate, seg, seg_before):
    length = steps.shape[0]
    running = exact_left(ones_where(row >= column), steps * rate, 3)
    entry = jnp.where(seg == seg_before[0:1], jnp.exp(running), 0.0)
    to_end = jnp.where(
        seg == seg[length - 1 : length], jnp.exp(running[length - 1 : length] - running), 0.0
    )
    return running, entry, to_end


def joined(pairs, second):
    count, _, width = pairs.shape
    begin = width // 2 if second else 0
    return jnp.concatenate(
        [pairs[i, :, begin : begin + width // 2] for i in range(count)], axis=1
    )


def state_kernel(values, pairs, steps, rate, seg, seg_before, state):
    length, width = values.shape
    heads = steps.shape[1]

    @pl.when(pl.program_id(0) == 0)
    def _():
        state[...] = jnp.zeros_like(state)

    row, column = span_index(length)
    expand = head_map(heads, width)
    step = steps[...]
    _, entry, to_end = decays(row, column, step, rate[...], seg[...], seg_before[...])
    weighted = exact_right(to_end * step, expand, 3) * values[...]
    kept = exact_right(jnp.broadcast_to(entry[length - 1 :], (8, heads)), expand, 3)[0:1]
    state[...] = kept * state[...] + exact_left(joined(pairs, False), weighted, 2, 0, 0)


def forward_kernel(
    values, pairs, steps, steps_row, rate, rate_row, seg, seg_row, seg_before, seg_group,
    skip, state_in, mixed, states, entries, state, total,
):
    length, width = values.shape
    heads = steps.shape[1]
    pair = 2 * (width // heads)

    @pl.when(pl.program_id(0) == 0)
    def _():
        state[...] = state_in[...]
        total[...] = jnp.zeros_like(total)

    row, column = span_index(length)
    expand = head_map(heads, width)
    step = steps[...]
    step_row = steps_row[...]
    running, entry, to_end = decays(row, column, step, rate[...], seg[...], seg_before[...])
    running_row = exact_right(step_row * rate_row[...], ones_where(row <= column), 3)
    same = (seg[...] == seg_row[...]) & (row >= column)
    write, read = joined(pairs, False), joined(pairs, True)
    scores = product(read, write, 1, 1)
    before = state[...]
    states[0] = before
    outer = exact_right(entry, expand, 3) * exact_left(read, before, 2)
    lane = lax.broadcasted_iota(jnp.int32, (length, pair), 1)
    for j in range(heads // 2):
        lanes = slice(j * pair, (j + 1) * pair)
        value = values[:, lanes]
        mixing = []
        for h in (2 * j, 2 * j + 1):
            gap = running[:, h : h + 1] - running_row[h : h + 1, :]
            mixing.append(
                jnp.exp(jnp.where(same, gap, -1e30)) * scores * step_row[h : h + 1, :]
            )
        stacked = jnp.concatenate(
            [jnp.where(lane < pair // 2, value, 0.0), jnp.where(lane >= pair // 2, value, 0.0)],
            axis=0,
        )
        mixed[:, lanes] = (
            split_product(jnp.concatenate(mixing, axis=1), stacked)
            + outer[:, lanes]
            + skip[:, lanes] * value
        )
    weighted = exact_right(to_end * step, expand, 3) * values[...]
    kept = exact_right(jnp.broadcast_to(entry[length - 1 :], (8, heads)), expand, 3)[0:1]
    state[...] = kept * before + exact_left(write, weighted, 2, 0, 0)
    whole = total[...] + running
    total[...] = whole[length - 1 :]
    entries[...] = exact_right(
        jnp.where(seg[...] == seg_group[...], jnp.exp(whole), 0.0), expand, 3
    )


def backward_kernel(
    values, grads, pairs, steps, steps_row, rate, rate_row, seg, seg_row, seg_before,
    skip, states, adjoint_in, values_grad, pairs_grad, steps_grad, decay_grad,
    skip_grad, adjoint,
):
    length, width = values.shape
    heads = steps.shape[1]
    pair = 2 * (width // heads)

    @pl.when(pl.program_id(0) == 0)
    def _():
        adjoint[...] = adjoint_in[...]
        decay_grad[...] = jnp.zeros_like(decay_grad)
        skip_grad[...] = jnp.zeros_like(skip_grad)

    row, column = span_index(length)
    expand = head_map(heads, width)
    step = steps[...]
    running, entry, to_end = decays(row, column, step, rate[...], seg[...], seg_before[...])
    running_row = exact_right(steps_row[...] * rate_row[...], ones_where(row <= column), 3)
    same = (seg[...] == seg_row[...]) & (row <= column)
    write, read = joined(pairs, False), joined(pairs, True)
    scores = product(write, read, 1, 1)
    later = adjoint[...]
    before = states[0]
    grad = grads[...]
    value = values[...]
    weight = to_end * step
    weights = exact_right(weight, expand, 3)
    entered = exact_right(entry, expand, 3) * grad
    arriving = exact_left(write, later, 2)
    scores_grad = jnp.zeros((length, length), jnp.float32)
    lane = lax.broadcasted_iota(jnp.int32, (length, pair), 1)
    head_lane = lax.broadcasted_iota(jnp.int32, (length, heads), 1)
    source_sums = jnp.zeros((length, heads), jnp.float32)
    target_sums = []
    for j in range(heads // 2):
        lanes = slice(j * pair, (j + 1) * pair)
        grad_pair = grads[:, lanes]
        value_pair = values[:, lanes]
        mixing = []
        halves = []
        for h in (2 * j, 2 * j + 1):
            mine = (lane < pair // 2) if h % 2 == 0 else (lane >= pair // 2)
            decay = jnp.exp(jnp.where(same, running_row[h : h + 1, :] - running[:, h : h + 1], -1e30))
            stepped = decay * step[:, h : h + 1]
            mixing.append(stepped * scores)
            mixing_grad = split_product(jnp.where(mine, value_pair, 0.0), grad_pair, 1, 1)
            stepped_grad = mixing_grad * stepped
            scores_grad = scores_grad + stepped_grad
            source = jnp.sum(mixing_grad * (decay * scores), axis=1, keepdims=True)
            source_sums = jnp.where(head_lane == h, source, source_sums)
            target_sums.append(jnp.sum(stepped_grad * scores, axis=0, keepdims=True))
            halves.append(jnp.where(mine, grad_pair, 0.0))
        values_grad[:, lanes] = (
            split_product(jnp.concatenate(mixing, axis=1), jnp.concatenate(halves, axis=0))
            + weights[:, lanes] * arriving[:, lanes]
            + skip[:, lanes] * grad_pair
        )
    target_rows = jnp.concatenate(target_sums, axis=0)
    targets = exact_left(ones_where(row == column), target_rows, 3, 1, 1)
    writes_grad = exact_right(scores_grad, read, 2) + split_product(
        weights * value, later, 1, 1
    )
    reads_grad = exact_right(scores_grad, write, 2, 0, 0) + split_product(
        entered, before, 1, 1
    )
    share = pairs.shape[2] // 2
    for i in range(pairs.shape[0]):
        mine = slice(i * share, (i + 1) * share)
        pairs_grad[i] = jnp.concatenate([writes_grad[:, mine], reads_grad[:, mine]], axis=1)
    inter = exact_right(entered * exact_left(read, before, 2), expand, 3, 1, 1)
    carried = exact_right(value * arriving, expand, 3, 1, 1)
    running_grad = targets + inter - source_sums * step - carried * weight
    state_sum = jnp.sum(later * before, axis=0, keepdims=True)
    state_heads = exact_right(jnp.broadcast_to(state_sum, (8, width)), expand, 3, 1, 1)[0:1]
    last = jnp.sum(carried * weight, axis=0, keepdims=True) + entry[length - 1 :] * state_heads
    logs_grad = exact_left(ones_where(row <= column), running_grad, 3) + last
    steps_grad[...] = source_sums + carried * to_end + logs_grad * rate[...]
    decay_grad[...] += jnp.sum(logs_grad * step * rate[...], axis=0, keepdims=True)
    skip_grad[...] += jnp.sum(grad * value, axis=0, keepdims=True)
    kept = exact_right(jnp.broadcast_to(entry[length - 1 :], (8, heads)), expand, 3)[0:1]
    adjoint[...] = kept * later + exact_left(read, entered, 2, 0, 0)


def scan_call(kernel, turns, reverse, operands, results, scratch, flops):
    def spec(shape, kind):
        def place(i):
            return turns - 1 - i if reverse else i

        if kind == "rows":
            return pl.BlockSpec((shape[0] // turns,) + shape[1:], lambda i: (place(i), 0))
        if kind == "columns":
            return pl.BlockSpec((shape[0], shape[1] // turns), lambda i: (0, place(i)))
        if kind == "parts":
            return pl.BlockSpec(
                (shape[0], shape[1] // turns, shape[2]), lambda i: (0, place(i), 0)
            )
        if kind == "turn":
            return pl.BlockSpec((1,) + shape[1:], lambda i: (place(i), 0, 0))
        return pl.BlockSpec(shape, lambda i: (0, 0))

    moved = sum(a.size * a.dtype.itemsize for a, _ in operands)
    return pl.pallas_call(
        kernel,
        grid=(turns,),
        in_specs=[spec(a.shape, kind) for a, kind in operands],
        out_specs=[spec(shape, kind) for shape, kind in results],
        out_shape=[jax.ShapeDtypeStruct(shape, jnp.float32) for shape, _ in results],
        scratch_shapes=[pltpu.VMEM(shape, jnp.float32) for shape in scratch],
        compiler_params=pltpu.CompilerParams(vmem_limit_bytes=40 * 1024 * 1024),
        cost_estimate=pl.CostEstimate(flops=flops, bytes_accessed=2 * moved, transcendentals=0),
    )(*[a for a, _ in operands])


def exchange_sum(blocks, axis):
    count = lax.axis_size(axis)
    place = lax.axis_index(axis)
    total = lax.dynamic_index_in_dim(blocks, place, 0, False).astype(jnp.float32)
    for hop in range(1, count):
        sent = lax.dynamic_index_in_dim(blocks, (place + hop) % count, 0, False)
        arrived = lax.ppermute(sent, axis, [(i, (i + hop) % count) for i in range(count)])
        total = total + arrived.astype(jnp.float32)
    return total


def exchange_rows(partial_sum, axis):
    count = lax.axis_size(axis)
    blocks = partial_sum.reshape((count, partial_sum.shape[0] // count) + partial_sum.shape[1:])
    return exchange_sum(blocks, axis)


def transfer_kernel(plan, *refs):
    count = len(plan)
    sources, targets = refs[:count], refs[count : 2 * count]
    send, receive, local = refs[2 * count :]
    axes = sorted({axis for axis, _ in plan})
    barrier = pltpu.get_barrier_semaphore()
    for axis in axes:
        size = lax.axis_size(axis)
        for hop in range(1, size):
            peer = lax.rem(lax.axis_index(axis) + hop, size)
            pl.semaphore_signal(
                barrier, inc=1, device_id={axis: peer}, device_id_type=pl.DeviceIdType.MESH
            )
    pl.semaphore_wait(barrier, sum(lax.axis_size(axis) - 1 for axis in axes))
    copies = []
    relays = []
    slot = 0

    def push(item, source, place, axis, peer, slot):
        return pltpu.make_async_remote_copy(
            src_ref=source,
            dst_ref=targets[item].at[place],
            send_sem=send.at[slot],
            recv_sem=receive.at[slot],
            device_id={axis: peer},
            device_id_type=pl.DeviceIdType.MESH,
        )

    for item, (axis, blocks) in enumerate(plan):
        size = lax.axis_size(axis)
        me = lax.axis_index(axis)
        paired = not blocks and axis == "dp" and size % 2 == 0
        for hop in (range(1, size) if not paired else range(2, size, 2)):
            peer = lax.rem(me + hop, size)
            copy = push(
                item, sources[item].at[peer] if blocks else sources[item], me, axis, peer, slot
            )
            copy.start()
            if paired:
                relays.append((copy, item, axis, lax.rem(me - hop + size, size), slot + 1))
                slot += 1
            copies.append(copy)
            slot += 1
        if paired:
            partner = me + 1 - 2 * lax.rem(me, 2)
            copy = push(item, sources[item], me, axis, partner, slot)
            copy.start()
            copies.append(copy)
            slot += 1
        own = pltpu.make_async_copy(
            sources[item].at[me] if blocks else sources[item], targets[item].at[me], local.at[item]
        )
        own.start()
        copies.append(own)
    for copy, item, axis, origin, place in relays:
        copy.wait_recv()
        me = lax.axis_index(axis)
        partner = me + 1 - 2 * lax.rem(me, 2)
        onward = push(item, targets[item].at[origin], origin, axis, partner, place)
        onward.start()
        copies.append(onward)
    relayed = [copy for copy, *_ in relays]
    for copy in copies:
        if any(copy is other for other in relayed):
            copy.wait_send()
        else:
            copy.wait()


def transfer(items, number):
    plan = tuple((axis, blocks) for _, axis, blocks in items)
    shapes = []
    slots = 0
    for array, axis, blocks in items:
        size = lax.axis_size(axis)
        shapes.append(
            jax.ShapeDtypeStruct(array.shape if blocks else (size,) + array.shape, array.dtype)
        )
        slots += size - 1
    return pl.pallas_call(
        partial(transfer_kernel, plan),
        in_specs=[pl.BlockSpec(memory_space=pl.ANY)] * len(items),
        out_specs=[pl.BlockSpec(memory_space=pl.ANY)] * len(items),
        out_shape=shapes,
        scratch_shapes=[
            pltpu.SemaphoreType.DMA((slots,)),
            pltpu.SemaphoreType.DMA((slots,)),
            pltpu.SemaphoreType.DMA((len(items),)),
        ],
        compiler_params=pltpu.CompilerParams(collective_id=number, has_side_effects=True),
    )(*[array for array, _, _ in items])


def blocks_of(array, axis):
    count = lax.axis_size(axis)
    return array.reshape((count, array.shape[0] // count) + array.shape[1:])


def total_of(arrived):
    return jnp.sum(arrived.astype(jnp.float32), axis=0)


def conv_apply(conv_in, rim, kernel, offset, valid):
    padded = jnp.concatenate([rim, conv_in], axis=0)
    group_rows = conv_in.shape[0]
    width = kernel.shape[0]
    total = offset[None, :]
    for tap_index in range(width):
        begin = width - 1 - tap_index
        total = total + kernel[tap_index][None, :] * jnp.where(
            valid[tap_index][:, None], padded[begin : begin + group_rows], 0.0
        )
    return jax.nn.silu(total)


def contract_last(left, right):
    return lax.dot_general(
        left, right, (((1,), (1,)), ((), ())), preferred_element_type=jnp.float32
    )


def contract_first(left, right):
    return lax.dot_general(
        left, right, (((0,), (0,)), ((), ())), preferred_element_type=jnp.float32
    )


def body(
    hidden_in,
    out_grad,
    seg_ids,
    norm_gain,
    gate_weight,
    value_weight,
    write_weight,
    read_weight,
    step_weight,
    step_bias,
    decay_log,
    skip_gain,
    conv_value,
    conv_write_read,
    conv_value_bias,
    conv_write_read_bias,
    gate_gain,
    out_weight,
):
    tensor_count = lax.axis_size("tensor")
    tensor_rank = lax.axis_index("tensor")
    data_rank = lax.axis_index("dp")
    own_rows = hidden_in.shape[0]
    group_rows = own_rows * tensor_count
    kernel_width = conv_value.shape[0]
    heads_here = step_weight.shape[1]
    inner_here = value_weight.shape[1]
    head_size = inner_here // heads_here
    state_here = write_weight.shape[1]
    state_size = state_here * tensor_count
    inner_total = inner_here * tensor_count
    gate_full, value_full, rest_full, hidden_rows = transfer(
        [
            (gate_weight, "dp", False),
            (value_weight, "dp", False),
            (jnp.concatenate([write_weight, read_weight, step_weight], axis=1), "dp", False),
            (hidden_in, "tensor", False),
        ],
        1,
    )
    gate_full, value_full, rest_full, hidden_rows = (
        item.reshape((-1, item.shape[2]))
        for item in (gate_full, value_full, rest_full, hidden_rows)
    )
    hidden_float = hidden_rows.astype(jnp.float32)
    scale = lax.rsqrt(jnp.mean(hidden_float * hidden_float, axis=1, keepdims=True) + epsilon)
    normed = hidden_float * scale
    features = (normed * norm_gain[None, :]).astype(jnp.bfloat16)
    gate_in = jnp.dot(features, gate_full, preferred_element_type=jnp.float32)
    value_in = jnp.dot(features, value_full, preferred_element_type=jnp.float32)
    rest_in = jnp.dot(features, rest_full, preferred_element_type=jnp.float32)
    pair_in, step_in = rest_in[:, : 2 * state_here], rest_in[:, 2 * state_here :]
    rim = from_behind(
        jnp.concatenate(
            [item[group_rows - (kernel_width - 1) :] for item in (value_in, pair_in)], axis=1
        ),
        "dp",
        1,
    )
    value_rim, pair_rim = rim[:, :inner_here], rim[:, inner_here:]
    pair_kernel = jnp.concatenate([conv_write_read[0], conv_write_read[1]], axis=1)
    pair_offset = conv_write_read_bias.reshape(-1)
    padded_seg = jnp.concatenate([jnp.full((kernel_width - 1,), -1, jnp.int32), seg_ids])
    window = lax.dynamic_slice_in_dim(
        padded_seg, data_rank * group_rows, group_rows + kernel_width - 1
    )
    segment = window[kernel_width - 1 :]
    valid = jnp.stack(
        [
            window[kernel_width - 1 - tap_index : kernel_width - 1 - tap_index + group_rows]
            == segment
            for tap_index in range(kernel_width)
        ]
    )
    convolve = partial(conv_apply, valid=valid)
    pair, pair_back = jax.vjp(convolve, pair_in, pair_rim, pair_kernel, pair_offset)
    values, value_back = jax.vjp(convolve, value_in, value_rim, conv_value, conv_value_bias)
    (pairs,) = transfer([(pair.astype(jnp.bfloat16), "tensor", False)], 2)
    grad_source, out_source, pairs = lax.optimization_barrier(
        (out_grad, out_weight, pairs)
    )
    grad_rows = lax.all_gather(grad_source, "tensor", axis=0, tiled=True)
    out_full = lax.all_gather(out_source, "dp", axis=0, tiled=True)
    steps = jax.nn.softplus(step_in + step_bias[None, :])
    rate = -jnp.exp(decay_log)
    turns = group_rows // SPAN
    steps_row = steps.T
    rates = (rate[None, :], "whole"), (rate[:, None], "whole")
    seg_column = (segment[:, None], "rows")
    seg_line = (segment[None, :], "columns")
    before = window[kernel_width - 2 : kernel_width - 2 + group_rows][:, None]
    skip = (jnp.repeat(skip_gain, head_size)[None, :], "whole")
    state_shape = (state_size, inner_here)
    (state_end,) = scan_call(
        state_kernel,
        turns,
        False,
        [
            (values, "rows"),
            (pairs, "parts"),
            (steps, "rows"),
            rates[0],
            seg_column,
            (before, "rows"),
        ],
        [(state_shape, "whole")],
        [],
        10**9,
    )
    state_in = from_behind(state_end, "dp", 1)
    shared = [
        (pairs, "parts"),
        (steps, "rows"),
        (steps_row, "columns"),
        *rates,
        seg_column,
        seg_line,
        (before, "rows"),
    ]
    mixed, states, entries = scan_call(
        forward_kernel,
        turns,
        False,
        [(values, "rows"), *shared, (before[:1], "whole"), skip, (state_in, "whole")],
        [
            (values.shape, "rows"),
            ((turns,) + state_shape, "turn"),
            (values.shape, "rows"),
        ],
        [state_shape, (1, heads_here)],
        10**10,
    )
    gate_act = jax.nn.silu(gate_in)
    gated = mixed * gate_act
    branch_grad = jnp.dot(grad_rows, out_full, preferred_element_type=jnp.float32)
    scaled = branch_grad * gate_gain[None, :]
    (token_sums,) = transfer(
        [
            (
                jnp.stack([jnp.sum(gated * gated, axis=1), jnp.sum(scaled * gated, axis=1)]),
                "tensor",
                False,
            )
        ],
        3,
    )
    squares, dots = total_of(token_sums)
    rms = lax.rsqrt(squares / inner_total + epsilon)
    branch = (gated * rms[:, None] * gate_gain[None, :]).astype(jnp.bfloat16)
    summed = exchange_rows(contract_last(branch, out_full).astype(jnp.bfloat16), "tensor")
    layer_out = hidden_in.astype(jnp.float32) + summed
    out_weight_grad = exchange_rows(contract_first(grad_rows, branch).astype(jnp.bfloat16), "dp")
    gate_gain_grad = jnp.sum(branch_grad * gated * rms[:, None], axis=0)
    gated_grad = rms[:, None] * scaled - gated * (rms * rms * rms * dots / inner_total)[:, None]
    mixed_grad = gated_grad * gate_act
    gate_sigmoid = jax.nn.sigmoid(gate_in)
    gate_grad = gated_grad * mixed * gate_sigmoid * (1.0 + gate_in * (1.0 - gate_sigmoid))
    carry_term = lax.dot_general(
        pairs[:, :, state_here:].transpose(1, 0, 2).reshape(group_rows, state_size).astype(jnp.float32),
        entries * mixed_grad,
        (((0,), (0,)), ((), ())),
        precision=highest,
    )
    adjoint_in = from_behind(carry_term, "dp", -1)
    values_grad, pairs_grad, steps_grad, decay_log_grad, skip_grad = scan_call(
        backward_kernel,
        turns,
        True,
        [
            (values, "rows"),
            (mixed_grad, "rows"),
            *shared,
            skip,
            (states, "turn"),
            (adjoint_in, "whole"),
        ],
        [
            (values.shape, "rows"),
            (pairs.shape, "parts"),
            (steps.shape, "rows"),
            ((1, heads_here), "whole"),
            ((1, inner_here), "whole"),
        ],
        [state_shape],
        2 * 10**10,
    )
    decay_log_grad = decay_log_grad[0]
    skip_grad = jnp.sum(skip_grad.reshape(heads_here, head_size), axis=1)
    pair_grad = exchange_sum(pairs_grad, "tensor")
    value_in_grad, value_rim_grad, value_kernel_grad, value_offset_grad = value_back(values_grad)
    pair_in_grad, pair_rim_grad, pair_kernel_grad, pair_offset_grad = pair_back(pair_grad)
    edge = group_rows - (kernel_width - 1)
    value_in_grad = value_in_grad.at[edge:].add(from_behind(value_rim_grad, "dp", -1))
    pair_in_grad = pair_in_grad.at[edge:].add(from_behind(pair_rim_grad, "dp", -1))
    step_pre = steps_grad * jax.nn.sigmoid(step_in + step_bias[None, :])
    step_bias_grad = jnp.sum(step_pre, axis=0)
    gate_low = gate_grad.astype(jnp.bfloat16)
    value_low = value_in_grad.astype(jnp.bfloat16)
    rest_low = jnp.concatenate([pair_in_grad, step_pre], axis=1).astype(jnp.bfloat16)
    features_grad = (
        contract_last(gate_low, gate_full)
        + contract_last(value_low, value_full)
        + contract_last(rest_low, rest_full)
    )
    gain_part = jnp.sum(features_grad * normed, axis=0)
    gate_share, value_share, rest_share = (
        blocks_of(contract_first(features, low).astype(jnp.bfloat16), "dp")
        for low in (gate_low, value_low, rest_low)
    )
    small = (
        gain_part,
        gate_gain_grad,
        step_bias_grad,
        decay_log_grad,
        skip_grad,
        value_kernel_grad,
        pair_kernel_grad,
        value_offset_grad,
        pair_offset_grad,
    )
    flat = jnp.concatenate([item.reshape(-1) for item in small])
    flat = jnp.pad(flat, (0, -flat.size % 1024)).reshape(-1, 128)
    features_parts, gate_parts, value_parts, rest_parts, flat_parts = transfer(
        [
            (blocks_of(features_grad.astype(jnp.bfloat16), "tensor"), "tensor", True),
            (gate_share, "dp", True),
            (value_share, "dp", True),
            (rest_share, "dp", True),
            (flat, "dp", False),
        ],
        4,
    )
    own_features_grad = total_of(features_parts)
    packed = total_of(flat_parts).reshape(-1)
    small_sums = []
    begin = 0
    for item in small:
        small_sums.append(packed[begin : begin + item.size].reshape(item.shape))
        begin += item.size
    (gain_parts,) = transfer(
        [(small_sums[0].reshape(tensor_count, 1, -1), "tensor", True)],
        5,
    )
    norm_gain_grad = total_of(gain_parts)[0]
    own_normed = lax.dynamic_slice_in_dim(normed, tensor_rank * own_rows, own_rows, 0)
    own_scale = lax.dynamic_slice_in_dim(scale, tensor_rank * own_rows, own_rows, 0)
    normed_grad = own_features_grad * norm_gain[None, :]
    input_grad = out_grad.astype(jnp.float32) + own_scale * (
        normed_grad - own_normed * jnp.mean(normed_grad * own_normed, axis=1, keepdims=True)
    )
    rest_sum = total_of(rest_parts)
    weight_sums = (
        total_of(gate_parts),
        total_of(value_parts),
        rest_sum[:, :state_here],
        rest_sum[:, state_here : 2 * state_here],
        rest_sum[:, 2 * state_here :],
        out_weight_grad,
    )

    def paired(array):
        return jnp.stack([array[..., :state_here], array[..., state_here:]])

    return (
        layer_out,
        input_grad,
        norm_gain_grad,
        weight_sums[0],
        weight_sums[1],
        weight_sums[2],
        weight_sums[3],
        weight_sums[4],
        small_sums[2],
        small_sums[3],
        small_sums[4],
        small_sums[5],
        paired(small_sums[6]),
        small_sums[7],
        paired(small_sums[8]),
        small_sums[1],
        weight_sums[5],
    )


def solution(mesh):
    return jax.shard_map(
        body,
        mesh=mesh,
        in_specs=(
            P(("dp", "tensor"), None),
            P(("dp", "tensor"), None),
            P(),
            P(),
            P("dp", "tensor"),
            P("dp", "tensor"),
            P("dp", "tensor"),
            P("dp", "tensor"),
            P("dp", "tensor"),
            P("tensor"),
            P("tensor"),
            P("tensor"),
            P(None, "tensor"),
            P(None, None, "tensor"),
            P("tensor"),
            P(None, "tensor"),
            P("tensor"),
            P("dp", "tensor"),
        ),
        out_specs=(
            P(("dp", "tensor"), None),
            P(("dp", "tensor"), None),
            P("tensor"),
            P("dp", "tensor"),
            P("dp", "tensor"),
            P("dp", "tensor"),
            P("dp", "tensor"),
            P("dp", "tensor"),
            P("tensor"),
            P("tensor"),
            P("tensor"),
            P(None, "tensor"),
            P(None, None, "tensor"),
            P("tensor"),
            P(None, "tensor"),
            P("tensor"),
            P("dp", "tensor"),
        ),
        check_vma=False,
    )
```
